512 devices in a mesh: adapter: 32 (over y, z_hi), tensor: 16 (over x, z_lo, core).
Axes of the slice: x: 4, y: 8, z: 8 (z_hi: 4, z_lo: 2; z = z_hi * 2 + z_lo), core: 2. Of those that a mesh axis runs over, the one named last changes fastest.
Arguments:
- residual_rows: bfloat16 [24576, 8192], P(('adapter', 'tensor')), may hold values from -6 to 6
- norm_gain_vector: bfloat16 [8192], replicated, may hold values from 0.099609375 to 1.8984375
- key_value_weight: bfloat16 [8192, 2048], P(None, 'tensor'), may hold values from -0.0625 to 0.0625
- adapter_down_weight: bfloat16 [256, 8192, 64], P('adapter', 'tensor'), may hold values from -0.0625 to 0.0625
- adapter_up_weight: bfloat16 [256, 64, 1024], P('adapter', None, 'tensor'), may hold values from -0.375 to 0.375
- request_adapter_index: int32 [6144, 1], P('adapter'), may hold values from 0 to 255, as said below
Outputs:
- projected: bfloat16 [24576, 2048], P('adapter', 'tensor')
The draws below stay inside these ranges and needn't reach their ends.
Inputs may be any that keep to these rules, and one draw needn't show every extreme that they name: `request_adapter_index`: among the 192 requests of one index of adapter (aligned blocks of rows), no adapter is named more than 3 times and some adapter exactly 3 times; adapters a with the same a // 8 are named at most 12 times together, and some such set exactly 12 times.
All inputs are finite; a program needn't handle non-finite values.
Results may differ from the reference program's by a relative error of at most 0.0055.
Values may be sent and summed in bfloat16 or wider, within the bound.
A program may use at most 64 MiB of HBM per device.

```python
import jax
import jax.numpy as jnp
from jax import lax

HIDDEN_WIDTH = 8192
KEY_VALUE_WIDTH = 1024
ADAPTER_RANK = 64
DRAFT = 4
REQ_G = 192
MOST = 3
DEST = 12
ADP_DEV = 8
ADAPTER_POOL = 256
REQUESTS = 6144
TOKENS = 24576
N_TENSOR = 16


def draw_request_adapter_index(key, part):
    key = jax.random.fold_in(key, 7)
    holders = ADAPTER_POOL // ADP_DEV
    slot_total = holders * DEST
    holder_order = jax.random.permutation(jax.random.fold_in(key, 1), holders)
    local_keys = jax.random.split(jax.random.fold_in(key, 2), holders)
    local_order = jax.vmap(lambda k: jax.random.permutation(k, ADP_DEV))(local_keys)

    def one_group(group):
        group_key = jax.random.fold_in(key, group + 100)
        position = jnp.arange(slot_total, dtype=jnp.int32)
        rank = position // DEST
        raw = jax.random.randint(jax.random.fold_in(group_key, 1), (slot_total,), 0, 4096)
        score = raw // (1 + rank) + jnp.where(rank == 0, 8192, 0)
        score = score * slot_total + (slot_total - 1 - position)
        unused, chosen = lax.top_k(score, REQ_G)
        holder = holder_order[chosen // DEST]
        local = local_order[holder, chosen % DEST // MOST]
        names = holder * ADP_DEV + local
        order = jax.random.permutation(jax.random.fold_in(group_key, 2), REQ_G)
        return names[order]
    result = jax.vmap(one_group)(jnp.arange(holders, dtype=jnp.int32))
    return result.reshape(-1, 1).astype(jnp.int32)


def level_of(own_key, extent, cuts, low, top_value):
    def one(axis_at, blocks):
        steps = jax.random.uniform(jax.random.fold_in(jax.random.fold_in(own_key, 6), axis_at), (blocks,), jnp.float32, low / len(cuts), top_value / len(cuts))
        return jnp.repeat(jnp.exp(steps), extent[axis_at] // blocks).reshape((-1,) + (1,) * (len(extent) - axis_at - 1))

    loudness = one(*cuts[0])
    for cut in cuts[1:]:
        loudness = loudness * one(*cut)
    return loudness


def gaussian(rng, dims, scale, reach, shards=(), kind=jnp.bfloat16):
    gain = level_of(rng, dims, shards, -0.22, 0.18) if shards else 1.0
    entries = jax.random.normal(rng, dims, jnp.float32) * scale * gain
    return jnp.minimum(jnp.maximum(entries, -reach), reach).astype(kind)


def setup_inputs(seed: int = 0) -> dict:
    splits = jax.random.split(jax.random.key(seed), 7)
    return {
        "residual_rows": gaussian(splits[0], (TOKENS, HIDDEN_WIDTH), 1.0, 6.0, ((0, 512),)),
        "norm_gain_vector": jnp.clip(1.0 + 0.18 * jax.random.normal(splits[1], (HIDDEN_WIDTH,), jnp.float32), 0.099609375, 1.8984375).astype(jnp.bfloat16),
        "key_value_weight": gaussian(splits[2], (HIDDEN_WIDTH, 2 * KEY_VALUE_WIDTH), HIDDEN_WIDTH ** -0.5, 0.0625, ((1, 16),)),
        "adapter_down_weight": gaussian(splits[3], (ADAPTER_POOL, HIDDEN_WIDTH, ADAPTER_RANK), HIDDEN_WIDTH ** -0.5, 0.0625, ((0, 32), (1, 16))),
        "adapter_up_weight": gaussian(splits[4], (ADAPTER_POOL, ADAPTER_RANK, KEY_VALUE_WIDTH), (4 * ADAPTER_RANK) ** -0.5, 0.375, ((0, 32), (2, 16))),
        "request_adapter_index": draw_request_adapter_index(jax.random.fold_in(splits[6], 71), 0),
    }


EPS = 1e-05
ADAPTER_SCALE = 2.0

def reference(residual_rows, norm_gain_vector, key_value_weight, adapter_down_weight, adapter_up_weight, request_adapter_index):
    values = residual_rows.astype(jnp.float32)
    inverse = lax.rsqrt(lax.optimization_barrier(jnp.mean(values * values, axis=-1, keepdims=True)) + EPS)
    normed = (values * inverse * norm_gain_vector.astype(jnp.float32)).astype(jnp.bfloat16)
    base = jnp.dot(normed, key_value_weight, preferred_element_type=jnp.float32)
    share = KEY_VALUE_WIDTH // N_TENSOR
    base = base.reshape(TOKENS, N_TENSOR, 2, share)
    grouped = normed.reshape(REQUESTS, DRAFT, HIDDEN_WIDTH)

    def per_request(item):
        rows, adapter_choice = item
        down_factor = adapter_down_weight[adapter_choice]
        up_factor = adapter_up_weight[adapter_choice]
        shrink_step = jnp.dot(rows, down_factor, preferred_element_type=jnp.float32).astype(jnp.bfloat16)
        return (jnp.dot(shrink_step, up_factor, preferred_element_type=jnp.float32) * ADAPTER_SCALE).astype(jnp.bfloat16)
    delta = lax.map(per_request, (grouped, request_adapter_index[:, 0]))
    delta = delta.reshape(TOKENS, N_TENSOR, share).astype(jnp.float32)
    keys = base[:, :, 0, :]
    vals = base[:, :, 1, :] + delta
    joined = jnp.stack([keys, vals], axis=2).astype(jnp.bfloat16)
    return joined.reshape(TOKENS, 2 * KEY_VALUE_WIDTH)
```

```python
import jax
import jax.numpy as jnp
from jax import lax
from jax.experimental import pallas as pl
from jax.experimental.pallas import tpu as pltpu
from jax.sharding import PartitionSpec as P

MESH = pl.DeviceIdType.MESH
F32 = jnp.float32
BF16 = jnp.bfloat16
I32 = jnp.int32

EPS = 1e-05
SCALE = 2.0

NY, NZH, NX, NT = 8, 4, 4, 16
ROWS = 48
GROUP = 768
REQS = 192
CAP = 192
HALF = CAP // 2
SHARE = 512
WIDTH = 8192
RANK = 64
HELD = 8

S_T, S_RS, S_SH = 0, 16, 32
S_YA, S_RET, S_IDX = 48, 56, 64
S_W, S_UP, S_AG, S_KV, S_BX = 72, 76, 80, 89, 90
N_SEM = 91


def iota(shape, dim):
    return lax.broadcasted_iota(I32, shape, dim)


def routing(tok):
    dest = lax.shift_right_logical(tok, 5)
    dest_f = dest.astype(F32)
    rr, cc = iota((REQS, GROUP), 0), iota((REQS, GROUP), 1)
    dest_col = jnp.sum(jnp.where(cc == rr * 4, dest_f, 0.0), axis=1, keepdims=True)
    earlier = (dest_col == dest_f) & (rr < lax.shift_right_logical(cc, 2))
    count = jnp.sum(jnp.where(earlier, 1.0, 0.0), axis=0, keepdims=True)
    slot = count.astype(I32) * 4 + (iota((1, GROUP), 1) & 3)
    return dest, slot


def chosen(dest, slot, row):
    return (slot == iota((CAP, GROUP), 0)) & (dest == row)


def order(n):
    return ((n + 1) // 2) * (2 * (n % 2) - 1)


def kernel(
    res_hbm, gain_ref, kv_hbm, down_hbm, up_hbm, tok_ref, out_ref,
    res, xa, xs, kvb, dn, wd, ups, upd, oh, oht, og, ig, tk, lidb,
    part, rsb, sh, dl, bown, bsib, bx, ssem, rsem, lsem,
):
    a = lax.axis_index("adapter")
    t = lax.axis_index("tensor")
    y, zh = a // NZH, a % NZH
    x, zl, c = t // 4, (t // 2) % 2, t % 2
    chip = t // 2

    def remote(src, dst, i, to):
        return pltpu.make_async_remote_copy(
            src_ref=src, dst_ref=dst, send_sem=ssem.at[i], recv_sem=rsem.at[i],
            device_id=to, device_id_type=MESH,
        )

    def arrived(dst, i):
        remote(dst, dst, i, (a, t)).wait_recv()

    def sent(src, i):
        remote(src, src, i, (a, t)).wait_send()

    def at_tensor(i):
        return (a, (t + i) % NT)

    def at_y(i):
        return (((y + i + NY) % NY) * NZH + zh, t)

    def at_z(i):
        return (y * NZH + (zh + i + NZH) % NZH, t)

    def at_x(i):
        return (a, ((x + i + NX) % NX) * 4 + zl * 2 + c)

    pair = (a, x * 4 + (1 - zl) * 2 + c)
    sibling = (a, t + 1 - 2 * c)

    def rows48(i):
        return pl.ds(pl.multiple_of(i * ROWS, 16), ROWS)

    local = [
        pltpu.make_async_copy(res_hbm, res, lsem.at[0]),
        pltpu.make_async_copy(kv_hbm, kvb.at[0], lsem.at[1]),
        pltpu.make_async_copy(down_hbm, dn, lsem.at[2]),
        pltpu.make_async_copy(up_hbm, ups, lsem.at[3]),
    ]
    for cp in local:
        cp.start()
    barrier = pltpu.get_barrier_semaphore()

    def greet(to):
        pl.semaphore_signal(barrier, inc=1, device_id=to, device_id_type=MESH)

    @pl.loop(1, NT)
    def _(i):
        greet(at_tensor(i))

    @pl.loop(1, NY)
    def _(i):
        greet(at_y(i))

    @pl.loop(1, NZH)
    def _(i):
        greet(at_z(i))

    mine = rows48(chip)
    local[0].wait()

    def squares(s, acc):
        v = res[:, pl.ds(pl.multiple_of(s * SHARE, SHARE), SHARE)].astype(F32)
        return acc + v * v

    total = lax.fori_loop(0, NT, squares, jnp.zeros((ROWS, SHARE), F32))
    inverse = lax.rsqrt(jnp.sum(total, axis=1, keepdims=True) * (1.0 / WIDTH) + EPS)

    @pl.loop(0, NT)
    def _(s):
        cols = pl.ds(pl.multiple_of(s * SHARE, SHARE), SHARE)
        v = res[:, cols].astype(F32) * inverse * gain_ref[:, cols].astype(F32)
        xa[s, mine, :] = v.astype(BF16)

    pl.semaphore_wait(barrier, NT + NY + NZH - 3)

    @pl.loop(1, NT)
    def _(i):
        p = (t + i) % NT
        remote(xa.at[p, mine, :], xs.at[rows48(t), :], S_T + i, (a, p)).start()

    xs[rows48(t), :] = xa[t, mine, :]
    local[1].wait()
    remote(kvb.at[0], kvb.at[1], S_KV, sibling).start()
    tk[y] = tok_ref[...]

    @pl.loop(1, NY)
    def _(i):
        remote(tok_ref, tk.at[y], S_IDX + i, at_y(i)).start()

    local[2].wait()
    for l in range(HELD):
        wd[zh, :, l * RANK : (l + 1) * RANK] = dn[l]
    local[3].wait()
    flat = ups[...].reshape(HELD * RANK, RANK)
    upd[zh, :, 0:RANK] = flat
    upd[zh, :, RANK : 2 * RANK] = flat

    tok = tok_ref[0:1, :]
    dest, slot = routing(tok)

    @pl.loop(0, NY)
    def _(d):
        oh[d] = jnp.where(chosen(dest, slot, d), 1.0, 0.0).astype(BF16)

    @pl.loop(1, NT)
    def _(i):
        arrived(xs.at[rows48((t - i + NT) % NT), :], S_T + i)

    @pl.loop(0, NY)
    def _(n):
        off = (4 + order(n) + NY) % NY
        d = (y + off) % NY
        og[d] = jnp.dot(oh[d], xs[...], preferred_element_type=F32).astype(BF16)

        @pl.when(off != 0)
        def _():
            remote(og.at[d], ig.at[y], S_YA + off, (d * NZH + zh, t)).start()

        @pl.when(off == 0)
        def _():
            ig[y] = og[d]

    def block(ix, iz):
        return rows48(((ix + NX) % NX) * 2 + iz)

    def hand_on(rows, i, to, first, many):
        ref = xa.at[pl.ds(first, many), rows, :]
        return remote(ref, ref, i, to)

    remote(wd.at[zh], wd.at[zh], S_W + 0, at_z(1)).start()
    remote(wd.at[zh], wd.at[zh], S_W + 1, at_z(-1)).start()
    hand_on(mine, S_AG + 0, pair, 0, NT).start()
    hand_on(mine, S_AG + 1, at_x(1), 0, NT).start()
    hand_on(mine, S_AG + 2, at_x(-1), 0, NT).start()
    for i in range(1, NZH):
        remote(upd.at[zh], upd.at[zh], S_UP + i, at_z(i)).start()

    place = dest * HALF + jnp.where(slot < HALF, slot, slot - HALF)
    code = (place + jnp.where(slot < HALF, 0, 1024)).astype(F32)
    rr, cc = iota((GROUP, GROUP), 0), iota((GROUP, GROUP), 1)
    code_col = jnp.sum(jnp.where(rr == cc, code, 0.0), axis=1, keepdims=True).astype(I32)
    oht[0] = jnp.where(code_col == cc, 1.0, 0.0).astype(BF16)
    oht[1] = jnp.where(code_col == cc + 1024, 1.0, 0.0).astype(BF16)

    @pl.loop(1, NY)
    def _(i):
        arrived(tk.at[(y - i + NY) % NY], S_IDX + i)

    @pl.loop(0, NY)
    def _(g):
        names = tk[g, 0:1, :]
        to_row, at_slot = routing(names)
        held = (names & (NZH * HELD - 1)).astype(F32)
        lid = jnp.sum(
            jnp.where(chosen(to_row, at_slot, y), held, 0.0), axis=1, keepdims=True
        )
        lidb[g] = jnp.broadcast_to(lid, (CAP, 128)).astype(I32)

    def base(ix):
        rows = pl.ds(pl.multiple_of(((ix + NX) % NX) * 2 * ROWS, 16), 2 * ROWS)

        def add(s, acc):
            ks = pl.ds(pl.multiple_of(s * SHARE, SHARE), SHARE)
            w = jnp.concatenate([kvb[0, ks, :], kvb[1, ks, :]], axis=1)
            return acc + jnp.dot(xa[s, rows, :], w, preferred_element_type=F32)

        acc = lax.fori_loop(0, NT, add, jnp.zeros((2 * ROWS, 256), F32))
        bown[rows, :] = acc[:, :128]
        bsib[rows, :] = acc[:, 128:]

    arrived(xa.at[:, block(x, 1 - zl), :], S_AG + 0)
    hand_on(block(x, 1 - zl), S_AG + 3, at_x(1), 0, NT).start()
    hand_on(block(x, 1 - zl), S_AG + 4, at_x(-1), 0, NT).start()
    arrived(kvb.at[1], S_KV)
    base(x)

    arrived(xa.at[:, block(x - 1, zl), :], S_AG + 1)
    hand_on(block(x - 1, zl), S_AG + 5, at_x(1), 0, NT // 2).start()
    arrived(xa.at[:, block(x + 1, zl), :], S_AG + 2)
    hand_on(block(x + 1, zl), S_AG + 6, at_x(-1), NT // 2, NT // 2).start()

    zp, zm = (zh + 1) % NZH, (zh + NZH - 1) % NZH
    arrived(wd.at[zm], S_W + 0)
    top, low = pl.ds(0, SHARE // 2), pl.ds(SHARE // 2, SHARE // 2)
    remote(wd.at[zm, top, :], wd.at[zm, top, :], S_W + 2, at_z(1)).start()
    arrived(wd.at[zp], S_W + 1)
    remote(wd.at[zp, low, :], wd.at[zp, low, :], S_W + 3, at_z(-1)).start()

    arrived(xa.at[:, block(x - 1, 1 - zl), :], S_AG + 3)
    hand_on(block(x - 1, 1 - zl), S_AG + 7, at_x(1), 0, NT // 2).start()
    arrived(xa.at[:, block(x + 1, 1 - zl), :], S_AG + 4)
    hand_on(block(x + 1, 1 - zl), S_AG + 8, at_x(-1), NT // 2, NT // 2).start()
    base(x - 1)
    base(x + 1)

    arrived(wd.at[zh, top, :], S_W + 2)
    arrived(wd.at[zh, low, :], S_W + 3)

    lane_low = iota((HALF, 128), 1) < RANK

    @pl.loop(0, NY)
    def _(n):
        off = (order(n) + NY) % NY
        g = (y - off + NY) % NY

        @pl.when(off != 0)
        def _():
            arrived(ig.at[g], S_YA + off)

        lid = lidb[g]
        lid2 = lax.shift_right_logical(lid, 1)
        rows = ig[g]
        acc = jnp.zeros((CAP, 128), F32)
        for q in range(NZH):
            prod = jnp.dot(rows, wd[q], preferred_element_type=F32)
            for k in range(4):
                acc = jnp.where(lid2 == q * 4 + k, prod[:, 128 * k : 128 * k + 128], acc)
        turned = pltpu.roll(acc, RANK, 1)
        odd = (lid & 1) == 1
        upper = jnp.where(odd[:HALF], turned[:HALF], acc[:HALF])
        lower = jnp.where(odd[HALF:], acc[HALF:], turned[HALF:])
        part[g] = jnp.where(lane_low, upper, lower)
        for h in range(2):
            p = g * 2 + h
            i = (p - t + NT) % NT

            @pl.when(i != 0)
            def _():
                remote(
                    part.at[g, pl.ds(h * ROWS, ROWS), :], rsb.at[t], S_RS + i, (a, p)
                ).start()

            @pl.when(i == 0)
            def _():
                rsb[t] = part[g, h * ROWS : (h + 1) * ROWS, :]

    @pl.loop(1, NT)
    def _(i):
        arrived(rsb.at[(t - i + NT) % NT], S_RS + i)

    def gather_sum(s, acc):
        return acc + rsb[s]

    shrunk = lax.fori_loop(0, NT, gather_sum, jnp.zeros((ROWS, 128), F32))
    sh[rows48(t), :] = shrunk.astype(BF16)

    @pl.loop(1, NT)
    def _(i):
        remote(sh.at[rows48(t), :], sh.at[rows48(t), :], S_SH + i, at_tensor(i)).start()

    for rows, i, half in (
        (block(x + 2, zl), 5, 0), (block(x + 2, zl), 6, 1),
        (block(x + 2, 1 - zl), 7, 0), (block(x + 2, 1 - zl), 8, 1),
    ):
        arrived(xa.at[pl.ds(half * NT // 2, NT // 2), rows, :], S_AG + i)
    base(x + 2)
    remote(bsib, bx, S_BX, sibling).start()
    for i in range(1, NZH):
        arrived(upd.at[(zh - i + NZH) % NZH], S_UP + i)

    lane_half = lax.shift_right_logical(iota((CAP, 128), 1), 6)

    @pl.loop(0, NY)
    def _(n):
        off = (order(n) + NY) % NY
        g = (y - off + NY) % NY
        for h in range(2):
            p = g * 2 + h
            i = (t - p + NT) % NT

            @pl.when(i != 0)
            def _():
                arrived(sh.at[rows48(p), :], S_SH + i)

        packed = sh[pl.ds(pl.multiple_of(g * HALF, 16), HALF), :].astype(F32)
        turned = pltpu.roll(packed, RANK, 1)
        both = jnp.concatenate(
            [jnp.where(lane_low, packed, turned), jnp.where(lane_low, turned, packed)], axis=0
        )
        key = lidb[g] - lane_half
        acc = jnp.zeros((CAP, 128), F32)
        for q in range(NZH):
            spread = jnp.concatenate(
                [jnp.where(key == q * 8 + 2 * k, both, 0.0).astype(BF16) for k in range(4)], axis=1
            )
            acc = acc + jnp.dot(spread, upd[q], preferred_element_type=F32)
        acc = acc * SCALE
        delta = jnp.where(lane_low, acc[:HALF], acc[HALF:]).astype(BF16)

        spot = pl.ds(pl.multiple_of(g * HALF, 16), HALF)
        part_out = og.at[g, pl.ds(0, HALF), pl.ds(0, 128)]

        @pl.when(off != 0)
        def _():
            sent(og.at[g], S_YA + (g - y + NY) % NY)
            part_out[...] = delta
            remote(
                part_out,
                dl.at[pl.ds(pl.multiple_of(y * HALF, 16), HALF), :],
                S_RET + (NY - off) % NY,
                (g * NZH + zh, t),
            ).start()

        @pl.when(off == 0)
        def _():
            dl[spot, :] = delta

    arrived(bx, S_BX)

    @pl.loop(1, NY)
    def _(i):
        arrived(dl.at[pl.ds(pl.multiple_of(((y - i + NY) % NY) * HALF, 16), HALF), :], S_RET + i)

    upper_lane = iota((2 * ROWS, 128), 1) >= RANK

    @pl.loop(0, NT // 2)
    def _(b):
        span = pl.ds(pl.multiple_of(b * 2 * ROWS, 16), 2 * ROWS)
        first = jnp.dot(oht[0, span, :], dl[...], preferred_element_type=F32)
        second = jnp.dot(oht[1, span, :], dl[...], preferred_element_type=F32)
        td = jnp.where(upper_lane, pltpu.roll(first, RANK, 1) + second, 0.0)
        own, other = bown[rows48(b), :], bx[rows48(b), :]
        low_part = jnp.where(c == 0, own, other)
        high_part = jnp.where(c == 0, other, own)
        both = jnp.concatenate([low_part, high_part], axis=0)
        out_ref[span, :] = (both + td).astype(BF16)

    @pl.loop(1, NT)
    def _(i):
        p = (t + i) % NT
        sent(xa.at[p, mine, :], S_T + i)
        sent(part.at[0, pl.ds(0, ROWS), :], S_RS + i)
        sent(sh.at[rows48(t), :], S_SH + i)

    @pl.loop(1, NY)
    def _(i):
        sent(tok_ref, S_IDX + i)
        sent(og.at[0, pl.ds(0, HALF), pl.ds(0, 128)], S_RET + i)

    sent(kvb.at[0], S_KV)
    sent(bsib, S_BX)
    sent(wd.at[zh], S_W + 0)
    sent(wd.at[zh], S_W + 1)
    sent(wd.at[zh, top, :], S_W + 2)
    sent(wd.at[zh, low, :], S_W + 3)
    for i in range(1, NZH):
        sent(upd.at[zh], S_UP + i)
    for i in range(5):
        sent(xa.at[:, mine, :], S_AG + i)
    for i in range(5, 9):
        sent(xa.at[pl.ds(0, NT // 2), mine, :], S_AG + i)


def per_device(residual, gain, kv, down, up, names):
    tok = jnp.broadcast_to(names.reshape(1, REQS, 1), (8, REQS, 4)).reshape(8, GROUP)
    any_spec = pl.BlockSpec(memory_space=pl.ANY)
    vmem = pl.BlockSpec(memory_space=pltpu.VMEM)
    V = pltpu.VMEM
    return pl.pallas_call(
        kernel,
        name="lora_kv",
        out_shape=jax.ShapeDtypeStruct((GROUP, 128), BF16),
        in_specs=[any_spec, vmem, any_spec, any_spec, any_spec, vmem],
        out_specs=vmem,
        scratch_shapes=[
            V((ROWS, WIDTH), BF16),
            V((NT, 8 * ROWS, SHARE), BF16),
            V((GROUP, SHARE), BF16),
            V((2, WIDTH, 128), BF16),
            V((HELD, SHARE, RANK), BF16),
            V((NZH, SHARE, HELD * RANK), BF16),
            V((HELD, RANK, RANK), BF16),
            V((NZH, HELD * RANK, 128), BF16),
            V((NY, CAP, GROUP), BF16),
            V((2, GROUP, GROUP), BF16),
            V((NY, CAP, SHARE), BF16),
            V((NY, CAP, SHARE), BF16),
            V((NY, 8, GROUP), I32),
            V((NY, CAP, 128), I32),
            V((NY, HALF, 128), F32),
            V((NT, ROWS, 128), F32),
            V((GROUP, 128), BF16),
            V((GROUP, 128), BF16),
            V((8 * ROWS, 128), F32),
            V((8 * ROWS, 128), F32),
            V((8 * ROWS, 128), F32),
            pltpu.SemaphoreType.DMA((N_SEM,)),
            pltpu.SemaphoreType.DMA((N_SEM,)),
            pltpu.SemaphoreType.DMA((4,)),
        ],
        compiler_params=pltpu.CompilerParams(
            collective_id=0, has_side_effects=True, vmem_limit_bytes=48 << 20
        ),
    )(residual, gain.reshape(1, WIDTH), kv, down, up, tok)


def solution(mesh):
    in_specs = (
        P(("adapter", "tensor"), None),
        P(),
        P(None, "tensor"),
        P("adapter", "tensor", None),
        P("adapter", None, "tensor"),
        P("adapter", None),
    )
    return jax.shard_map(
        per_device,
        mesh=mesh,
        in_specs=in_specs,
        out_specs=P("adapter", "tensor"),
        check_vma=False,
    )
```

```python
import jax
import jax.numpy as jnp
from jax import lax
from jax.experimental import pallas as pl
from jax.experimental.pallas import tpu as pltpu
from jax.sharding import PartitionSpec as P

MESH = pl.DeviceIdType.MESH
F32 = jnp.float32
BF16 = jnp.bfloat16
I32 = jnp.int32

EPS = 1e-05
SCALE = 2.0

NY, NZH, NX, NT = 8, 4, 4, 16
ROWS = 48
GROUP = 768
REQS = 192
CAP = 192
HALF = CAP // 2
SHARE = 512
WIDTH = 8192
RANK = 64
HELD = 8

S_T, S_RS, S_SH = 0, 32, 48
S_YA, S_RET, S_IDX = 64, 80, 88
S_W, S_UP, S_AG, S_XB, S_KV, S_BX = 96, 102, 106, 115, 123, 124
N_SEM = 125


def iota(shape, dim):
    return lax.broadcasted_iota(I32, shape, dim)


def routing(tok):
    dest = lax.shift_right_logical(tok, 5)
    dest_f = dest.astype(F32)
    rr, cc = iota((REQS, GROUP), 0), iota((REQS, GROUP), 1)
    dest_col = jnp.sum(jnp.where(cc == rr * 4, dest_f, 0.0), axis=1, keepdims=True)
    earlier = (dest_col == dest_f) & (rr < lax.shift_right_logical(cc, 2))
    count = jnp.sum(jnp.where(earlier, 1.0, 0.0), axis=0, keepdims=True)
    slot = count.astype(I32) * 4 + (iota((1, GROUP), 1) & 3)
    return dest, slot


def chosen(dest, slot, row):
    return (slot == iota((CAP, GROUP), 0)) & (dest == row)


def order(n):
    return ((n + 1) // 2) * (2 * (n % 2) - 1)


def packed_rows(acc, lid):
    low = iota((HALF, 128), 1) < RANK
    turned = pltpu.roll(acc, RANK, 1)
    odd = (lid & 1) == 1
    upper = jnp.where(odd[:HALF], turned[:HALF], acc[:HALF])
    lower = jnp.where(odd[HALF:], acc[HALF:], turned[HALF:])
    return jnp.where(low, upper, lower)


def kernel(
    res_hbm, gain_ref, kv_hbm, down_hbm, up_hbm, names_ref, out_ref,
    res, xa, xb, xc, xs, kvb, dn, wd, ups, upd, oh, oht, og, ig, delta, tk, lidb,
    part, rsb, sh, dl, bown, bsend, bx, ssem, rsem, lsem,
):
    a = lax.axis_index("adapter")
    t = lax.axis_index("tensor")
    y, zh = a // NZH, a % NZH
    x, zl, c = t // 4, (t // 2) % 2, t % 2
    j = x * 2 + c

    def remote(src, dst, i, to):
        return pltpu.make_async_remote_copy(
            src_ref=src, dst_ref=dst, send_sem=ssem.at[i], recv_sem=rsem.at[i],
            device_id=to, device_id_type=MESH,
        )

    def arrived(dst, i):
        remote(dst, dst, i, (a, t)).wait_recv()

    def sent(src, i):
        remote(src, src, i, (a, t)).wait_send()

    def at_tensor(i):
        return (a, (t + i) % NT)

    def at_y(i):
        return (((y + i + NY) % NY) * NZH + zh, t)

    def at_z(i):
        return (y * NZH + (zh + i + NZH) % NZH, t)

    def tensor_of(p, plane):
        return (p // 2) * 4 + plane * 2 + p % 2

    def at_x(i):
        return (a, ((x + i + NX) % NX) * 4 + zl * 2 + c)

    pair = (a, x * 4 + (1 - zl) * 2 + c)
    sibling = (a, t + 1 - 2 * c)

    def rows48(i):
        return pl.ds(pl.multiple_of(i * ROWS, 16), ROWS)

    def block(ix):
        return rows48((ix + NX) % NX)

    def half_cols(h):
        return pl.ds(h * (SHARE // 2), SHARE // 2)

    spot_t = (zl * 2 + c) * 4 + x

    mine = rows48(x)

    local = [
        pltpu.make_async_copy(res_hbm, res, lsem.at[0]),
        pltpu.make_async_copy(kv_hbm, kvb.at[0], lsem.at[1]),
        pltpu.make_async_copy(down_hbm, dn, lsem.at[2]),
        pltpu.make_async_copy(up_hbm, ups, lsem.at[3]),
    ]
    for cp in local:
        cp.start()
    barrier = pltpu.get_barrier_semaphore()

    def greet(to):
        pl.semaphore_signal(barrier, inc=1, device_id=to, device_id_type=MESH)

    @pl.loop(1, NT)
    def _(i):
        greet(at_tensor(i))

    @pl.loop(1, NY)
    def _(i):
        greet(at_y(i))

    @pl.loop(1, NZH)
    def _(i):
        greet(at_z(i))

    local[0].wait()

    def squares(s, acc):
        v = res[:, pl.ds(pl.multiple_of(s * SHARE, SHARE), SHARE)].astype(F32)
        return acc + v * v

    total = lax.fori_loop(0, NT, squares, jnp.zeros((ROWS, SHARE), F32))
    inverse = lax.rsqrt(jnp.sum(total, axis=1, keepdims=True) * (1.0 / WIDTH) + EPS)

    @pl.loop(0, NT)
    def _(s):
        cols = pl.ds(pl.multiple_of(tensor_of(s % 8, s // 8) * SHARE, SHARE), SHARE)
        v = res[:, cols].astype(F32) * inverse * gain_ref[cols].astype(F32).reshape(1, SHARE)
        xa[s, mine, :] = v.astype(BF16)

    pl.semaphore_wait(barrier, NT + NY + NZH - 3)

    def hand_on(buf, rows, i, to, first, many):
        ref = buf.at[pl.ds(first, many), rows, :]
        return remote(ref, ref, i, to)

    def send_shares(h):
        @pl.loop(1, NT)
        def _(i):
            s = (zl * 8 + j + i) % NT
            p = tensor_of(s % 8, s // 8)
            remote(
                xa.at[s, mine, half_cols(h)], xs.at[rows48(spot_t), half_cols(h)], S_T + 16 * h + i, (a, p)
            ).start()

    send_shares(0)
    send_shares(1)
    hand_on(xa, mine, S_AG + 0, at_x(1), 0, NT).start()
    hand_on(xa, mine, S_AG + 1, at_x(-1), 0, NT).start()
    remote(xa.at[pl.ds(zl * 8, 8), mine, :], xc.at[:, mine, :], S_AG + 4, pair).start()
    xs[rows48(spot_t), :] = xa[zl * 8 + j, mine, :]

    names = jnp.broadcast_to(names_ref[...].astype(F32), (8, REQS)).astype(BF16)
    rr, cc = iota((REQS, GROUP), 0), iota((REQS, GROUP), 1)
    lane_spot = lax.shift_right_logical(lax.shift_right_logical(cc, 4) * 171, 9)
    lane_dev = (lane_spot & 3) * 4 + lax.shift_right_logical(lane_spot, 2)
    request = lane_dev * (ROWS // 4) + lax.shift_right_logical(cc - lane_spot * ROWS, 2)
    fourfold = jnp.where(rr == request, 1.0, 0.0).astype(BF16)
    tk[y] = jnp.dot(names, fourfold, preferred_element_type=F32).astype(I32)

    @pl.loop(1, NY)
    def _(i):
        remote(tk.at[y], tk.at[y], S_IDX + i, at_y(i)).start()

    local[1].wait()
    remote(kvb.at[0], kvb.at[1], S_KV, sibling).start()

    dest, slot = routing(tk[y, 0:1, :])

    @pl.loop(0, NY)
    def _(d):
        oh[d] = jnp.where(chosen(dest, slot, d), 1.0, 0.0).astype(BF16)

    def send_rows(h):
        @pl.loop(1, NT)
        def _(i):
            arrived(xs.at[rows48(0), half_cols(h)], S_T + 16 * h + i)

        @pl.loop(0, NY)
        def _(n):
            off = (4 + order(n) + NY) % NY
            d = (y + off) % NY
            og[d, :, half_cols(h)] = jnp.dot(
                oh[d], xs[:, half_cols(h)], preferred_element_type=F32
            ).astype(BF16)

            @pl.when(off != 0)
            def _():
                remote(
                    og.at[d, :, half_cols(h)], ig.at[y, :, half_cols(h)],
                    S_YA + 8 * h + off, (d * NZH + zh, t),
                ).start()

            @pl.when(off == 0)
            def _():
                ig[y, :, half_cols(h)] = og[d, :, half_cols(h)]

    local[2].wait()
    wd[zh] = dn[...].reshape(HELD * RANK, SHARE).T
    local[3].wait()
    for l in range(HELD):
        upd[zh, :, l * RANK : (l + 1) * RANK] = ups[l]

    send_rows(0)

    send_rows(1)

    top, low = pl.ds(0, SHARE // 2), pl.ds(SHARE // 2, SHARE // 2)

    def weights_on(q, part_of, i, to):
        ref = wd.at[(q + NZH) % NZH, part_of, :]
        remote(ref, ref, S_W + i, at_z(to)).start()

    weights_on(zh, top, 0, 1)
    weights_on(zh, low, 1, -1)
    weights_on(zh, low, 2, 1)
    weights_on(zh, top, 3, -1)


    def other_rows(core):
        return pl.ds(pl.multiple_of(((1 - zl) * 2 + core) * 4 * ROWS, 16), 4 * ROWS)

    @pl.loop(1, 8)
    def _(i):
        p = (j + i) % 8
        remote(
            xs.at[other_rows(p % 2), :], xb.at[j], S_XB + i, (a, tensor_of(p, zl))
        ).start()

    xb[j] = xs[other_rows(c), :]

    @pl.loop(1, NY)
    def _(i):
        arrived(tk.at[(y - i + NY) % NY], S_IDX + i)

    @pl.loop(0, NY)
    def _(g):
        their = tk[g, 0:1, :]
        to_row, at_slot = routing(their)
        held = (their & (NZH * HELD - 1)).astype(F32)
        lid = jnp.sum(
            jnp.where(chosen(to_row, at_slot, y), held, 0.0), axis=1, keepdims=True
        )
        lidb[g] = jnp.broadcast_to(lid, (CAP, 128)).astype(I32)

    arrived(wd.at[zh, top, :], S_W + 0)
    weights_on(zh - 1, top, 4, 1)
    arrived(wd.at[zh, low, :], S_W + 1)
    weights_on(zh + 1, low, 5, -1)

    for i in range(1, NZH):
        remote(upd.at[zh], upd.at[zh], S_UP + i, at_z(i)).start()


    arrived(xa.at[:, block(x - 1), :], S_AG + 0)
    hand_on(xa, block(x - 1), S_AG + 2, at_x(1), 0, 8).start()
    arrived(xa.at[:, block(x + 1), :], S_AG + 1)
    hand_on(xa, block(x + 1), S_AG + 3, at_x(-1), 8, 8).start()

    place = dest * HALF + jnp.where(slot < HALF, slot, slot - HALF)
    code = (place + jnp.where(slot < HALF, 0, 1024)).astype(F32)
    rr, cc = iota((GROUP, GROUP), 0), iota((GROUP, GROUP), 1)
    code_col = jnp.sum(jnp.where(rr == cc, code, 0.0), axis=1, keepdims=True).astype(I32)
    oht[0] = jnp.where(code_col == cc, 1.0, 0.0).astype(BF16)
    oht[1] = jnp.where(code_col == cc + 1024, 1.0, 0.0).astype(BF16)

    def weights(s):
        ks = pl.ds(pl.multiple_of(tensor_of(s % 8, s // 8) * SHARE, SHARE), SHARE)
        return jnp.concatenate([kvb[0, ks, :], kvb[1, ks, :]], axis=1)

    def base(buf, plane, many, at, fresh):
        at = pl.ds(pl.multiple_of(at * 4 * ROWS, 16), 4 * ROWS)

        def add(s, acc):
            return acc + jnp.dot(buf[s], weights(plane * 8 + s), preferred_element_type=F32)

        acc = lax.fori_loop(0, many, add, jnp.zeros((4 * ROWS, 256), F32))
        if fresh:
            bown[at, :] = acc[:, :128]
            bsend[at, :] = acc[:, 128:]
        else:
            bown[at, :] = bown[at, :] + acc[:, :128]
            bsend[at, :] = bsend[at, :] + acc[:, 128:]

    arrived(xc.at[:, mine, :], S_AG + 4)
    hand_on(xc, mine, S_AG + 5, at_x(1), 0, 8).start()
    hand_on(xc, mine, S_AG + 6, at_x(-1), 0, 8).start()

    arrived(kvb.at[1], S_KV)
    arrived(xa.at[pl.ds(0, 8), block(x + 2), :], S_AG + 2)
    arrived(xa.at[pl.ds(8, 8), block(x + 2), :], S_AG + 3)
    base(xa, 0, NT, zl, True)

    @pl.loop(1, 8)
    def _(i):
        arrived(xb.at[0], S_XB + i)

    base(xb, zl, 8, 1 - zl, True)

    for i in range(2, 6):
        arrived(wd.at[zh, top, :], S_W + i)
    for i in range(1, NZH):
        arrived(upd.at[(zh - i + NZH) % NZH], S_UP + i)

    lane_low = iota((HALF, 128), 1) < RANK

    def source(n):
        off = (order(n) + NY) % NY
        return off, (y - off + NY) % NY

    def shrink(n):
        off, g = source(n)

        @pl.when(off != 0)
        def _():
            for h in range(2):
                arrived(ig.at[g, :, half_cols(h)], S_YA + 8 * h + off)

        lid = lidb[g]
        lid2 = lax.shift_right_logical(lid, 1)
        rows = ig[g]
        acc = jnp.zeros((CAP, 128), F32)
        for q in range(NZH):
            prod = jnp.dot(rows, wd[q], preferred_element_type=F32)
            for k in range(4):
                acc = jnp.where(lid2 == q * 4 + k, prod[:, 128 * k : 128 * k + 128], acc)
        part[g] = packed_rows(acc, lid)
        for h in range(2):
            p = g * 2 + h
            i = (p - t + NT) % NT

            @pl.when(i != 0)
            def _():
                remote(
                    part.at[g, pl.ds(h * ROWS, ROWS), :], rsb.at[t], S_RS + i, (a, p)
                ).start()

            @pl.when(i == 0)
            def _():
                rsb[t] = part[g, h * ROWS : (h + 1) * ROWS, :]

    def own_sum():
        @pl.loop(1, NT)
        def _(i):
            arrived(rsb.at[(t - i + NT) % NT], S_RS + i)

        shrunk = lax.fori_loop(
            0, NT, lambda s, acc: acc + rsb[s], jnp.zeros((ROWS, 128), F32)
        )
        sh[rows48(t), :] = shrunk.astype(BF16)

        @pl.loop(1, NT)
        def _(i):
            remote(sh.at[rows48(t), :], sh.at[rows48(t), :], S_SH + i, at_tensor(i)).start()

    def expand(n):
        off, g = source(n)
        for h in range(2):
            p = g * 2 + h
            i = (t - p + NT) % NT

            @pl.when(i != 0)
            def _():
                arrived(sh.at[rows48(p), :], S_SH + i)

        spot = pl.ds(pl.multiple_of(g * HALF, 16), HALF)
        packed = sh[spot, :].astype(F32)
        each = jnp.concatenate(
            [jnp.where(lane_low, packed, 0.0), jnp.where(lane_low, 0.0, packed)], axis=0
        ).astype(BF16)
        lid = lidb[g]
        lid2 = lax.shift_right_logical(lid, 1)
        acc = jnp.zeros((CAP, 128), F32)
        for q in range(NZH):
            twice = jnp.concatenate([upd[q], upd[q]], axis=0)
            prod = jnp.dot(each, twice, preferred_element_type=F32)
            for k in range(4):
                acc = jnp.where(lid2 == q * 4 + k, prod[:, 128 * k : 128 * k + 128], acc)
        delta[g] = (packed_rows(acc, lid) * SCALE).astype(BF16)

        @pl.when(off != 0)
        def _():
            remote(
                delta.at[g],
                dl.at[pl.ds(pl.multiple_of(y * HALF, 16), HALF), :],
                S_RET + (NY - off) % NY,
                (g * NZH + zh, t),
            ).start()

        @pl.when(off == 0)
        def _():
            dl[spot, :] = delta[g]

    apart = (y - t // 2 + NY) % NY
    beyond = apart // 5
    turn = (1 - beyond) * (2 * apart - 1 + (4 - apart) // 4) + beyond * 2 * (NY - apart)

    LATE, LATER = 3, 5

    @pl.loop(0, NY + LATER)
    def _(n):
        @pl.when(n < NY)
        def _():
            shrink(n)

        @pl.when(n == 6)
        def _():
            arrived(xc.at[:, block(x - 1), :], S_AG + 5)
            hand_on(xc, block(x - 1), S_AG + 7, at_x(1), 0, 4).start()
            arrived(xc.at[:, block(x + 1), :], S_AG + 6)
            hand_on(xc, block(x + 1), S_AG + 8, at_x(-1), 4, 4).start()

        @pl.when(n == turn + LATE)
        def _():
            own_sum()

        @pl.when(n >= LATER)
        def _():
            expand(n - LATER)

    arrived(xc.at[pl.ds(0, 4), block(x + 2), :], S_AG + 7)
    arrived(xc.at[pl.ds(4, 4), block(x + 2), :], S_AG + 8)
    base(xc, 1 - zl, 8, 1 - zl, False)
    remote(bsend, bx, S_BX, sibling).start()

    @pl.loop(1, NY)
    def _(i):
        arrived(dl.at[pl.ds(pl.multiple_of(((y - i + NY) % NY) * HALF, 16), HALF), :], S_RET + i)

    arrived(bx, S_BX)

    upper_lane = iota((4 * ROWS, 128), 1) >= RANK

    @pl.loop(0, 4)
    def _(b):
        span = pl.ds(pl.multiple_of(b * 4 * ROWS, 16), 4 * ROWS)
        first = jnp.dot(oht[0, span, :], dl[...], preferred_element_type=F32)
        second = jnp.dot(oht[1, span, :], dl[...], preferred_element_type=F32)
        td = jnp.where(upper_lane, pltpu.roll(first, RANK, 1) + second, 0.0)
        rows = pl.ds(pl.multiple_of((b // 2) * 4 * ROWS, 16), 4 * ROWS)
        value = jnp.where(b % 2 == c, bown[rows, :], bx[rows, :]) + td
        for ix in range(NX):
            out_ref[rows48(ix * 4 + b), :] = value[ix * ROWS : (ix + 1) * ROWS].astype(BF16)

    @pl.loop(1, NT)
    def _(i):
        for h in range(2):
            sent(xa.at[0, mine, half_cols(h)], S_T + 16 * h + i)
        sent(part.at[0, pl.ds(0, ROWS), :], S_RS + i)
        sent(sh.at[rows48(t), :], S_SH + i)

    @pl.loop(1, NY)
    def _(i):
        sent(tk.at[y], S_IDX + i)
        sent(delta.at[0], S_RET + i)
        for h in range(2):
            sent(og.at[0, :, half_cols(h)], S_YA + 8 * h + i)
        sent(xb.at[0], S_XB + i)

    sent(kvb.at[0], S_KV)
    sent(bsend, S_BX)
    sent(xa.at[:, mine, :], S_AG + 0)
    sent(xa.at[:, mine, :], S_AG + 1)
    for i in (2, 3, 4, 5, 6):
        sent(xc.at[:, mine, :], S_AG + i)
    for i in (7, 8):
        sent(xc.at[pl.ds(0, 4), mine, :], S_AG + i)
    for i in range(6):
        sent(wd.at[zh, top, :], S_W + i)
    for i in range(1, NZH):
        sent(upd.at[zh], S_UP + i)


def per_device(residual, gain, kv, down, up, names):
    hbm = pl.BlockSpec(memory_space=pltpu.HBM)
    vmem = pl.BlockSpec(memory_space=pltpu.VMEM)
    V = pltpu.VMEM
    return pl.pallas_call(
        kernel,
        name="lora_kv",
        out_shape=jax.ShapeDtypeStruct((GROUP, 128), BF16),
        in_specs=[hbm, vmem, hbm, hbm, hbm, vmem],
        out_specs=vmem,
        scratch_shapes=[
            V((ROWS, WIDTH), BF16),
            V((NT, NX * ROWS, SHARE), BF16),
            V((8, NX * ROWS, SHARE), BF16),
            V((8, NX * ROWS, SHARE), BF16),
            V((GROUP, SHARE), BF16),
            V((2, WIDTH, 128), BF16),
            V((HELD, RANK, SHARE), BF16),
            V((NZH, SHARE, HELD * RANK), BF16),
            V((HELD, RANK, RANK), BF16),
            V((NZH, RANK, HELD * RANK), BF16),
            V((NY, CAP, GROUP), BF16),
            V((2, GROUP, GROUP), BF16),
            V((NY, CAP, SHARE), BF16),
            V((NY, CAP, SHARE), BF16),
            V((NY, HALF, 128), BF16),
            V((NY, 8, GROUP), I32),
            V((NY, CAP, 128), I32),
            V((NY, HALF, 128), F32),
            V((NT, ROWS, 128), F32),
            V((GROUP, 128), BF16),
            V((GROUP, 128), BF16),
            V((GROUP // 2, 128), F32),
            V((GROUP // 2, 128), F32),
            V((GROUP // 2, 128), F32),
            pltpu.SemaphoreType.DMA((N_SEM,)),
            pltpu.SemaphoreType.DMA((N_SEM,)),
            pltpu.SemaphoreType.DMA((4,)),
        ],
        compiler_params=pltpu.CompilerParams(
            collective_id=0, has_side_effects=True, vmem_limit_bytes=63 << 20
        ),
    )(residual, gain, kv, jnp.swapaxes(down, 1, 2), up, names.reshape(1, REQS))


def solution(mesh):
    in_specs = (
        P(("adapter", "tensor"), None),
        P(),
        P(None, "tensor"),
        P("adapter", "tensor", None),
        P("adapter", None, "tensor"),
        P("adapter", None),
    )
    return jax.shard_map(
        per_device,
        mesh=mesh,
        in_specs=in_specs,
        out_specs=P("adapter", "tensor"),
        check_vma=False,
    )
```

```python
import jax
import jax.numpy as jnp
from jax import lax
from jax.experimental import pallas as pl
from jax.experimental.pallas import tpu as pltpu
from jax.sharding import PartitionSpec as P

MESH = pl.DeviceIdType.MESH
F32 = jnp.float32
BF16 = jnp.bfloat16
I32 = jnp.int32

EPS = 1e-05
SCALE = 2.0

NY, NZH, NX, NT = 8, 4, 4, 16
ROWS = 48
GROUP = 768
REQS = 192
CAP = 192
HALF = CAP // 2
SHARE = 512
WIDTH = 8192
RANK = 64
HELD = 8

S_T, S_RS, S_SH = 0, 32, 48
S_YA, S_RET, S_IDX = 64, 80, 88
S_W, S_UP, S_AG, S_XB, S_KV, S_BX = 96, 102, 106, 115, 123, 124
N_SEM = 125


def iota(shape, dim):
    return lax.broadcasted_iota(I32, shape, dim)


def routing(tok):
    dest = lax.shift_right_logical(tok, 5)
    dest_f = dest.astype(F32)
    rr, cc = iota((REQS, GROUP), 0), iota((REQS, GROUP), 1)
    dest_col = jnp.sum(jnp.where(cc == rr * 4, dest_f, 0.0), axis=1, keepdims=True)
    earlier = (dest_col == dest_f) & (rr < lax.shift_right_logical(cc, 2))
    count = jnp.sum(jnp.where(earlier, 1.0, 0.0), axis=0, keepdims=True)
    slot = count.astype(I32) * 4 + (iota((1, GROUP), 1) & 3)
    return dest, slot


def chosen(dest, slot, row):
    return (slot == iota((CAP, GROUP), 0)) & (dest == row)


def order(n):
    return ((n + 7) // 8) * (4 - n // 2) * (1 - 2 * (n % 2))


def packed_rows(acc, lid):
    low = iota((HALF, 128), 1) < RANK
    turned = pltpu.roll(acc, RANK, 1)
    odd = (lid & 1) == 1
    upper = jnp.where(odd[:HALF], turned[:HALF], acc[:HALF])
    lower = jnp.where(odd[HALF:], acc[HALF:], turned[HALF:])
    return jnp.where(low, upper, lower)


def kernel(
    res_hbm, gain_hbm, kv_hbm, down_hbm, up_hbm, names_hbm, out_ref,
    res, gain_ref, names_ref, xa, xb, xc, xs, kvb, dn, wd, ups, upd, up2, mask, oh, oht, og, ig, delta, tk, lidb,
    part, rsb, sh, dl, bown, bsend, bx, ssem, rsem, lsem,
):
    a = lax.axis_index("adapter")
    t = lax.axis_index("tensor")
    y, zh = a // NZH, a % NZH
    x, zl, c = t // 4, (t // 2) % 2, t % 2
    j = x * 2 + c

    def remote(src, dst, i, to):
        return pltpu.make_async_remote_copy(
            src_ref=src, dst_ref=dst, send_sem=ssem.at[i], recv_sem=rsem.at[i],
            device_id=to, device_id_type=MESH,
        )

    def arrived(dst, i):
        remote(dst, dst, i, (a, t)).wait_recv()

    def sent(src, i):
        remote(src, src, i, (a, t)).wait_send()

    def at_tensor(i):
        return (a, (t + i) % NT)

    def at_y(i):
        return (((y + i + NY) % NY) * NZH + zh, t)

    def at_z(i):
        return (y * NZH + (zh + i + NZH) % NZH, t)

    def tensor_of(p, plane):
        return (p // 2) * 4 + plane * 2 + p % 2

    def at_x(i):
        return (a, ((x + i + NX) % NX) * 4 + zl * 2 + c)

    pair = (a, x * 4 + (1 - zl) * 2 + c)
    sibling = (a, t + 1 - 2 * c)

    def rows48(i):
        return pl.ds(pl.multiple_of(i * ROWS, 16), ROWS)

    def block(ix):
        return rows48((ix + NX) % NX)

    def half_cols(h):
        return pl.ds(h * (SHARE // 2), SHARE // 2)

    spot_t = (zl * 2 + c) * 4 + x

    mine = rows48(x)

    local = [
        pltpu.make_async_copy(res_hbm, res, lsem.at[0]),
        pltpu.make_async_copy(gain_hbm, gain_ref, lsem.at[4]),
        pltpu.make_async_copy(names_hbm, names_ref, lsem.at[5]),
        pltpu.make_async_copy(kv_hbm, kvb.at[0], lsem.at[1]),
        pltpu.make_async_copy(down_hbm, dn, lsem.at[2]),
        pltpu.make_async_copy(up_hbm, ups, lsem.at[3]),
    ]
    for cp in local:
        cp.start()
    barrier = pltpu.get_barrier_semaphore()

    def greet(to):
        pl.semaphore_signal(barrier, inc=1, device_id=to, device_id_type=MESH)

    @pl.loop(1, NT)
    def _(i):
        greet(at_tensor(i))

    @pl.loop(1, NY)
    def _(i):
        greet(at_y(i))

    @pl.loop(1, NZH)
    def _(i):
        greet(at_z(i))

    local[0].wait()
    local[1].wait()
    local[2].wait()

    def squares(s, acc):
        v = res[:, pl.ds(pl.multiple_of(s * SHARE, SHARE), SHARE)].astype(F32)
        return acc + v * v

    total = lax.fori_loop(0, NT, squares, jnp.zeros((ROWS, SHARE), F32))
    inverse = lax.rsqrt(jnp.sum(total, axis=1, keepdims=True) * (1.0 / WIDTH) + EPS)

    def normalise(s):
        cols = pl.ds(pl.multiple_of(tensor_of(s % 8, s // 8) * SHARE, SHARE), SHARE)
        v = res[:, cols].astype(F32) * inverse * gain_ref[cols].astype(F32).reshape(1, SHARE)
        xa[s, mine, :] = v.astype(BF16)

    pl.semaphore_wait(barrier, NT + NY + NZH - 3)

    def hand_on(buf, rows, i, to, first, many):
        ref = buf.at[pl.ds(first, many), rows, :]
        return remote(ref, ref, i, to)

    def send_shares(h):
        @pl.loop(1, NT)
        def _(i):
            s = (zl * 8 + j + i) % NT
            if h == 0:
                normalise(s)
            p = tensor_of(s % 8, s // 8)
            remote(
                xa.at[s, mine, half_cols(h)], xs.at[rows48(spot_t), half_cols(h)], S_T + 16 * h + i, (a, p)
            ).start()

    send_shares(0)
    normalise(zl * 8 + j)
    send_shares(1)
    hand_on(xa, mine, S_AG + 0, at_x(1), 0, NT).start()
    hand_on(xa, mine, S_AG + 1, at_x(-1), 0, NT).start()
    remote(xa.at[pl.ds(zl * 8, 8), mine, :], xc.at[:, mine, :], S_AG + 4, pair).start()
    xs[rows48(spot_t), :] = xa[zl * 8 + j, mine, :]

    names = jnp.broadcast_to(names_ref[...].astype(F32), (8, REQS)).astype(BF16)
    rr, cc = iota((REQS, GROUP), 0), iota((REQS, GROUP), 1)
    lane_spot = lax.shift_right_logical(lax.shift_right_logical(cc, 4) * 171, 9)
    lane_dev = (lane_spot & 3) * 4 + lax.shift_right_logical(lane_spot, 2)
    request = lane_dev * (ROWS // 4) + lax.shift_right_logical(cc - lane_spot * ROWS, 2)
    fourfold = jnp.where(rr == request, 1.0, 0.0).astype(BF16)
    tk[y] = jnp.dot(names, fourfold, preferred_element_type=F32).astype(I32)

    @pl.loop(1, NY)
    def _(i):
        remote(tk.at[y], tk.at[y], S_IDX + i, at_y(i)).start()

    local[3].wait()
    remote(kvb.at[0], kvb.at[1], S_KV, sibling).start()

    dest, slot = routing(tk[y, 0:1, :])

    @pl.loop(0, NY)
    def _(d):
        oh[d] = jnp.where(chosen(dest, slot, d), 1.0, 0.0).astype(BF16)

    def send_rows(h):
        @pl.loop(1, NT)
        def _(i):
            arrived(xs.at[rows48(0), half_cols(h)], S_T + 16 * h + i)

        @pl.loop(0, NY)
        def _(n):
            off = (order(n) + NY) % NY
            d = (y + off) % NY
            og[d, :, half_cols(h)] = jnp.dot(
                oh[d], xs[:, half_cols(h)], preferred_element_type=F32
            ).astype(BF16)

            @pl.when((n >= 1) & (n <= 3))
            def _():
                remote(
                    og.at[d, :, half_cols(h)], ig.at[y, :, half_cols(h)],
                    S_YA + 8 * h + off, (d * NZH + zh, t),
                ).start()

            @pl.when(off == 0)
            def _():
                ig[y, :, half_cols(h)] = og[d, :, half_cols(h)]

    local[4].wait()
    wd[zh] = dn[...].reshape(HELD * RANK, SHARE).T
    local[5].wait()
    for l in range(HELD):
        upd[zh, :, l * RANK : (l + 1) * RANK] = ups[l]

    top, low = pl.ds(0, SHARE // 2), pl.ds(SHARE // 2, SHARE // 2)

    def weights_on(q, part_of, i, to):
        ref = wd.at[(q + NZH) % NZH, part_of, :]
        remote(ref, ref, S_W + i, at_z(to)).start()

    weights_on(zh, top, 0, 1)
    weights_on(zh, low, 1, -1)
    weights_on(zh, low, 2, 1)
    weights_on(zh, top, 3, -1)

    send_rows(0)

    send_rows(1)


    def other_rows(core):
        return pl.ds(pl.multiple_of(((1 - zl) * 2 + core) * 4 * ROWS, 16), 4 * ROWS)

    @pl.loop(1, 8)
    def _(i):
        p = (j + i) % 8
        remote(
            xs.at[other_rows(p % 2), :], xb.at[j], S_XB + i, (a, tensor_of(p, zl))
        ).start()

    xb[j] = xs[other_rows(c), :]

    @pl.loop(1, NY)
    def _(i):
        arrived(tk.at[(y - i + NY) % NY], S_IDX + i)

    @pl.loop(0, NY)
    def _(g):
        their = tk[g, 0:1, :]
        to_row, at_slot = routing(their)
        held = (their & (NZH * HELD - 1)).astype(F32)
        lid = jnp.sum(
            jnp.where(chosen(to_row, at_slot, y), held, 0.0), axis=1, keepdims=True
        )
        wide = jnp.broadcast_to(lid, (CAP, 128)).astype(I32)
        lidb[g] = wide
        key = wide - lax.shift_right_logical(iota((CAP, 128), 1), 6)
        for k in range(NZH * 4):
            mask[g, k] = jnp.where(key == 2 * k, 1.0, 0.0).astype(BF16)

    arrived(wd.at[zh, top, :], S_W + 0)
    weights_on(zh - 1, top, 4, 1)
    arrived(wd.at[zh, low, :], S_W + 1)
    weights_on(zh + 1, low, 5, -1)

    for i in range(1, NZH):
        remote(upd.at[zh], upd.at[zh], S_UP + i, at_z(i)).start()


    for h in range(2):
        for off in (4, 3, 5):
            sent(og.at[0, :, half_cols(h)], S_YA + 8 * h + off)
    for off in (2, 6, 1, 7):
        d = (y + off) % NY
        remote(og.at[d], ig.at[y], S_YA + off, (d * NZH + zh, t)).start()

    arrived(xa.at[:, block(x - 1), :], S_AG + 0)
    hand_on(xa, block(x - 1), S_AG + 2, at_x(1), 0, 8).start()
    arrived(xa.at[:, block(x + 1), :], S_AG + 1)
    hand_on(xa, block(x + 1), S_AG + 3, at_x(-1), 8, 8).start()

    place = dest * HALF + jnp.where(slot < HALF, slot, slot - HALF)
    code = (place + jnp.where(slot < HALF, 0, 1024)).astype(F32)
    rr, cc = iota((GROUP, GROUP), 0), iota((GROUP, GROUP), 1)
    code_col = jnp.sum(jnp.where(rr == cc, code, 0.0), axis=1, keepdims=True).astype(I32)
    oht[0] = jnp.where(code_col == cc, 1.0, 0.0).astype(BF16)
    oht[1] = jnp.where(code_col == cc + 1024, 1.0, 0.0).astype(BF16)

    def weights(s):
        ks = pl.ds(pl.multiple_of(tensor_of(s % 8, s // 8) * SHARE, SHARE), SHARE)
        return jnp.concatenate([kvb[0, ks, :], kvb[1, ks, :]], axis=1)

    def base(buf, plane, many, at, fresh):
        at = pl.ds(pl.multiple_of(at * 4 * ROWS, 16), 4 * ROWS)

        def add(s, acc):
            return acc + jnp.dot(buf[s], weights(plane * 8 + s), preferred_element_type=F32)

        acc = lax.fori_loop(0, many, add, jnp.zeros((4 * ROWS, 256), F32))
        if fresh:
            bown[at, :] = acc[:, :128]
            bsend[at, :] = acc[:, 128:]
        else:
            bown[at, :] = bown[at, :] + acc[:, :128]
            bsend[at, :] = bsend[at, :] + acc[:, 128:]

    arrived(xc.at[:, mine, :], S_AG + 4)
    hand_on(xc, mine, S_AG + 5, at_x(1), 0, 8).start()
    hand_on(xc, mine, S_AG + 6, at_x(-1), 0, 8).start()

    arrived(kvb.at[1], S_KV)
    arrived(xa.at[pl.ds(0, 8), block(x + 2), :], S_AG + 2)
    arrived(xa.at[pl.ds(8, 8), block(x + 2), :], S_AG + 3)
    base(xa, 0, NT, zl, True)

    for i in range(2, 6):
        arrived(wd.at[zh, top, :], S_W + i)

    lane_low = iota((HALF, 128), 1) < RANK

    def source(n):
        off = (order(n) + NY) % NY
        return off, (y - off + NY) % NY

    def shrink(n):
        off, g = source(n)

        @pl.when((n >= 1) & (n <= 3))
        def _():
            for h in range(2):
                arrived(ig.at[g, :, half_cols(h)], S_YA + 8 * h + off)

        @pl.when(n >= 4)
        def _():
            arrived(ig.at[g], S_YA + off)

        lid = lidb[g]
        lid2 = lax.shift_right_logical(lid, 1)
        rows = ig[g]
        acc = jnp.zeros((CAP, 128), F32)
        for q in range(NZH):
            prod = jnp.dot(rows, wd[q], preferred_element_type=F32)
            for k in range(4):
                acc = jnp.where(lid2 == q * 4 + k, prod[:, 128 * k : 128 * k + 128], acc)
        part[g] = packed_rows(acc, lid).astype(BF16)
        for h in range(2):
            p = g * 2 + h
            i = (p - t + NT) % NT

            @pl.when(i != 0)
            def _():
                remote(
                    part.at[g, pl.ds(h * ROWS, ROWS), :], rsb.at[t], S_RS + i, (a, p)
                ).start()

            @pl.when(i == 0)
            def _():
                rsb[t] = part[g, h * ROWS : (h + 1) * ROWS, :]

    def own_sum():
        @pl.loop(1, NT)
        def _(i):
            arrived(rsb.at[(t - i + NT) % NT], S_RS + i)

        shrunk = lax.fori_loop(
            0, NT, lambda s, acc: acc + rsb[s].astype(F32), jnp.zeros((ROWS, 128), F32)
        )
        sh[rows48(t), :] = shrunk.astype(BF16)

        @pl.loop(1, NT)
        def _(i):
            remote(sh.at[rows48(t), :], sh.at[rows48(t), :], S_SH + i, at_tensor(i)).start()

    def expand(n):
        off, g = source(n)
        for h in range(2):
            p = g * 2 + h
            i = (t - p + NT) % NT

            @pl.when(i != 0)
            def _():
                arrived(sh.at[rows48(p), :], S_SH + i)

        spot = pl.ds(pl.multiple_of(g * HALF, 16), HALF)
        packed = sh[spot, :].astype(F32)
        turned = pltpu.roll(packed, RANK, 1)
        both = jnp.concatenate(
            [jnp.where(lane_low, packed, turned), jnp.where(lane_low, turned, packed)], axis=0
        ).astype(BF16)
        acc = jnp.zeros((CAP, 128), F32)
        for q in range(NZH):
            spread = jnp.concatenate([both * mask[g, q * 4 + k] for k in range(4)], axis=1)
            acc = acc + jnp.dot(spread, up2[q], preferred_element_type=F32)
        acc = acc * SCALE
        delta[g] = jnp.where(lane_low, acc[:HALF], acc[HALF:]).astype(BF16)

        @pl.when(off != 0)
        def _():
            remote(
                delta.at[g],
                dl.at[pl.ds(pl.multiple_of(y * HALF, 16), HALF), :],
                S_RET + (NY - off) % NY,
                (g * NZH + zh, t),
            ).start()

        @pl.when(off == 0)
        def _():
            dl[spot, :] = delta[g]

    apart = (y - t // 2 + NY) % NY
    beyond = apart // 4
    turn = beyond * (2 * apart - 7) + (1 - beyond) * (8 - 2 * apart) - 8 * ((7 - apart) // 7)
    LATE, LATER = 3, 5

    @pl.loop(0, NY + LATER)
    def _(n):
        @pl.when(n < NY)
        def _():
            shrink(n)

        @pl.when(n == 6)
        def _():
            arrived(xc.at[:, block(x - 1), :], S_AG + 5)
            hand_on(xc, block(x - 1), S_AG + 7, at_x(1), 0, 4).start()
            arrived(xc.at[:, block(x + 1), :], S_AG + 6)
            hand_on(xc, block(x + 1), S_AG + 8, at_x(-1), 4, 4).start()

        @pl.when(n == NY)
        def _():
            @pl.loop(1, 8)
            def _(i):
                arrived(xb.at[0], S_XB + i)

            base(xb, zl, 8, 1 - zl, True)

        @pl.when(n == turn + LATE - (turn // 6) * (turn - 5))
        def _():
            own_sum()

        @pl.when(n == LATER)
        def _():
            for i in range(1, NZH):
                arrived(upd.at[(zh - i + NZH) % NZH], S_UP + i)
            for q in range(NZH):
                for l in range(HELD):
                    piece = upd[q, :, l * RANK : (l + 1) * RANK]
                    up2[q, l * RANK : (l + 1) * RANK, 0:RANK] = piece
                    up2[q, l * RANK : (l + 1) * RANK, RANK : 2 * RANK] = piece

        @pl.when(n >= LATER)
        def _():
            expand(n - LATER)

    arrived(xc.at[pl.ds(0, 4), block(x + 2), :], S_AG + 7)
    arrived(xc.at[pl.ds(4, 4), block(x + 2), :], S_AG + 8)
    base(xc, 1 - zl, 8, 1 - zl, False)
    remote(bsend, bx, S_BX, sibling).start()

    @pl.loop(1, NY)
    def _(i):
        arrived(dl.at[pl.ds(pl.multiple_of(((y - i + NY) % NY) * HALF, 16), HALF), :], S_RET + i)

    arrived(bx, S_BX)

    upper_lane = iota((4 * ROWS, 128), 1) >= RANK

    @pl.loop(0, 4)
    def _(b):
        span = pl.ds(pl.multiple_of(b * 4 * ROWS, 16), 4 * ROWS)
        first = jnp.dot(oht[0, span, :], dl[...], preferred_element_type=F32)
        second = jnp.dot(oht[1, span, :], dl[...], preferred_element_type=F32)
        td = jnp.where(upper_lane, pltpu.roll(first, RANK, 1) + second, 0.0)
        rows = pl.ds(pl.multiple_of((b // 2) * 4 * ROWS, 16), 4 * ROWS)
        value = jnp.where(b % 2 == c, bown[rows, :], bx[rows, :]) + td
        for ix in range(NX):
            out_ref[rows48(ix * 4 + b), :] = value[ix * ROWS : (ix + 1) * ROWS].astype(BF16)

    @pl.loop(1, NT)
    def _(i):
        for h in range(2):
            sent(xa.at[0, mine, half_cols(h)], S_T + 16 * h + i)
        sent(part.at[0, pl.ds(0, ROWS), :], S_RS + i)
        sent(sh.at[rows48(t), :], S_SH + i)

    @pl.loop(1, NY)
    def _(i):
        sent(tk.at[y], S_IDX + i)
        sent(delta.at[0], S_RET + i)
        sent(xb.at[0], S_XB + i)

    for off in (1, 2, 6, 7):
        sent(og.at[0], S_YA + off)
    sent(kvb.at[0], S_KV)
    sent(bsend, S_BX)
    sent(xa.at[:, mine, :], S_AG + 0)
    sent(xa.at[:, mine, :], S_AG + 1)
    for i in (2, 3, 4, 5, 6):
        sent(xc.at[:, mine, :], S_AG + i)
    for i in (7, 8):
        sent(xc.at[pl.ds(0, 4), mine, :], S_AG + i)
    for i in range(6):
        sent(wd.at[zh, top, :], S_W + i)
    for i in range(1, NZH):
        sent(upd.at[zh], S_UP + i)


def per_device(residual, gain, kv, down, up, names):
    hbm = pl.BlockSpec(memory_space=pltpu.HBM)
    vmem = pl.BlockSpec(memory_space=pltpu.VMEM)
    V = pltpu.VMEM
    return pl.pallas_call(
        kernel,
        name="lora_kv",
        out_shape=jax.ShapeDtypeStruct((GROUP, 128), BF16),
        in_specs=[hbm] * 6,
        out_specs=vmem,
        scratch_shapes=[
            V((ROWS, WIDTH), BF16),
            V((WIDTH,), BF16),
            V((1, REQS), I32),
            V((NT, NX * ROWS, SHARE), BF16),
            V((8, NX * ROWS, SHARE), BF16),
            V((8, NX * ROWS, SHARE), BF16),
            V((GROUP, SHARE), BF16),
            V((2, WIDTH, 128), BF16),
            V((HELD, RANK, SHARE), BF16),
            V((NZH, SHARE, HELD * RANK), BF16),
            V((HELD, RANK, RANK), BF16),
            V((NZH, RANK, HELD * RANK), BF16),
            V((NZH, HELD * RANK, 128), BF16),
            V((NY, NZH * 4, CAP, 128), BF16),
            V((NY, CAP, GROUP), BF16),
            V((2, GROUP, GROUP), BF16),
            V((NY, CAP, SHARE), BF16),
            V((NY, CAP, SHARE), BF16),
            V((NY, HALF, 128), BF16),
            V((NY, 8, GROUP), I32),
            V((NY, CAP, 128), I32),
            V((NY, HALF, 128), BF16),
            V((NT, ROWS, 128), BF16),
            V((GROUP, 128), BF16),
            V((GROUP, 128), BF16),
            V((GROUP // 2, 128), F32),
            V((GROUP // 2, 128), F32),
            V((GROUP // 2, 128), F32),
            pltpu.SemaphoreType.DMA((N_SEM,)),
            pltpu.SemaphoreType.DMA((N_SEM,)),
            pltpu.SemaphoreType.DMA((6,)),
        ],
        compiler_params=pltpu.CompilerParams(
            collective_id=0, has_side_effects=True, vmem_limit_bytes=63 << 20
        ),
    )(residual, gain, kv, jnp.swapaxes(down, 1, 2), up, names.reshape(1, REQS))


def solution(mesh):
    in_specs = (
        P(("adapter", "tensor"), None),
        P(),
        P(None, "tensor"),
        P("adapter", "tensor", None),
        P("adapter", None, "tensor"),
        P("adapter", None),
    )
    return jax.shard_map(
        per_device,
        mesh=mesh,
        in_specs=in_specs,
        out_specs=P("adapter", "tensor"),
        check_vma=False,
    )
```

```python
import jax
import jax.numpy as jnp
from jax import lax
from jax.experimental import pallas as pl
from jax.experimental.pallas import tpu as pltpu
from jax.sharding import PartitionSpec as P

MESH = pl.DeviceIdType.MESH
F32 = jnp.float32
BF16 = jnp.bfloat16
I32 = jnp.int32

EPS = 1e-05
SCALE = 2.0

NY, NZH, NX, NT = 8, 4, 4, 16
ROWS = 48
GROUP = 768
REQS = 192
CAP = 192
HALF = CAP // 2
SHARE = 512
WIDTH = 8192
RANK = 64
HELD = 8

S_T, S_RS, S_SH = 0, 32, 48
S_YA, S_RET, S_IDX = 64, 80, 88
S_W, S_UP, S_AG, S_XB, S_KV, S_BX = 96, 102, 106, 115, 123, 124
N_SEM = 125


def iota(shape, dim):
    return lax.broadcasted_iota(I32, shape, dim)


def routing(tok):
    dest = lax.shift_right_logical(tok, 5)
    dest_f = dest.astype(F32)
    rr, cc = iota((REQS, GROUP), 0), iota((REQS, GROUP), 1)
    dest_col = jnp.sum(jnp.where(cc == rr * 4, dest_f, 0.0), axis=1, keepdims=True)
    earlier = (dest_col == dest_f) & (rr < lax.shift_right_logical(cc, 2))
    count = jnp.sum(jnp.where(earlier, 1.0, 0.0), axis=0, keepdims=True)
    slot = count.astype(I32) * 4 + (iota((1, GROUP), 1) & 3)
    return dest, slot


def chosen(dest, slot, row):
    return (slot == iota((CAP, GROUP), 0)) & (dest == row)


def order(n):
    return ((n + 7) // 8) * (4 - n // 2) * (1 - 2 * (n % 2))


def packed_rows(acc, lid):
    low = iota((HALF, 128), 1) < RANK
    turned = pltpu.roll(acc, RANK, 1)
    odd = (lid & 1) == 1
    upper = jnp.where(odd[:HALF], turned[:HALF], acc[:HALF])
    lower = jnp.where(odd[HALF:], acc[HALF:], turned[HALF:])
    return jnp.where(low, upper, lower)


def kernel(
    res_hbm, gain_hbm, kv_hbm, down_hbm, up_hbm, names_hbm, out_ref,
    res, gain_ref, names_ref, xa, xb, xc, xs, kvb, dn, wd, ups, upd, up2, mask, oh, oht, og, ig, delta, tk, lidb,
    part, rsb, sh, dl, bown, bsend, bx, ssem, rsem, lsem,
):
    a = lax.axis_index("adapter")
    t = lax.axis_index("tensor")
    y, zh = a // NZH, a % NZH
    x, zl, c = t // 4, (t // 2) % 2, t % 2
    j = x * 2 + c

    def remote(src, dst, i, to):
        return pltpu.make_async_remote_copy(
            src_ref=src, dst_ref=dst, send_sem=ssem.at[i], recv_sem=rsem.at[i],
            device_id=to, device_id_type=MESH,
        )

    def arrived(dst, i):
        remote(dst, dst, i, (a, t)).wait_recv()

    def sent(src, i):
        remote(src, src, i, (a, t)).wait_send()

    def at_tensor(i):
        return (a, (t + i) % NT)

    def at_y(i):
        return (((y + i + NY) % NY) * NZH + zh, t)

    def at_z(i):
        return (y * NZH + (zh + i + NZH) % NZH, t)

    def tensor_of(p, plane):
        return (p // 2) * 4 + plane * 2 + p % 2

    def at_x(i):
        return (a, ((x + i + NX) % NX) * 4 + zl * 2 + c)

    pair = (a, x * 4 + (1 - zl) * 2 + c)
    sibling = (a, t + 1 - 2 * c)

    def rows48(i):
        return pl.ds(pl.multiple_of(i * ROWS, 16), ROWS)

    def block(ix):
        return rows48((ix + NX) % NX)

    def half_cols(h):
        return pl.ds(h * (SHARE // 2), SHARE // 2)

    spot_t = (zl * 2 + c) * 4 + x

    mine = rows48(x)

    local = [
        pltpu.make_async_copy(res_hbm, res, lsem.at[0]),
        pltpu.make_async_copy(gain_hbm, gain_ref, lsem.at[4]),
        pltpu.make_async_copy(names_hbm, names_ref, lsem.at[5]),
        pltpu.make_async_copy(kv_hbm, kvb.at[0], lsem.at[1]),
        pltpu.make_async_copy(down_hbm, dn, lsem.at[2]),
        pltpu.make_async_copy(up_hbm, ups, lsem.at[3]),
    ]
    for cp in local:
        cp.start()
    barrier = pltpu.get_barrier_semaphore()

    def greet(to):
        pl.semaphore_signal(barrier, inc=1, device_id=to, device_id_type=MESH)

    @pl.loop(1, NT)
    def _(i):
        greet(at_tensor(i))

    @pl.loop(1, NY)
    def _(i):
        greet(at_y(i))

    @pl.loop(1, NZH)
    def _(i):
        greet(at_z(i))

    local[0].wait()
    local[1].wait()
    local[2].wait()

    def squares(s, acc):
        v = res[:, pl.ds(pl.multiple_of(s * SHARE, SHARE), SHARE)].astype(F32)
        return acc + v * v

    total = lax.fori_loop(0, NT, squares, jnp.zeros((ROWS, SHARE), F32))
    inverse = lax.rsqrt(jnp.sum(total, axis=1, keepdims=True) * (1.0 / WIDTH) + EPS)

    def normalise(s):
        cols = pl.ds(pl.multiple_of(tensor_of(s % 8, s // 8) * SHARE, SHARE), SHARE)
        v = res[:, cols].astype(F32) * inverse * gain_ref[cols].astype(F32).reshape(1, SHARE)
        xa[s, mine, :] = v.astype(BF16)

    pl.semaphore_wait(barrier, NT + NY + NZH - 3)

    def hand_on(buf, rows, i, to, first, many):
        ref = buf.at[pl.ds(first, many), rows, :]
        return remote(ref, ref, i, to)

    def send_shares(h):
        @pl.loop(1, NT)
        def _(i):
            s = (zl * 8 + j + i) % NT
            if h == 0:
                normalise(s)
            p = tensor_of(s % 8, s // 8)
            remote(
                xa.at[s, mine, half_cols(h)], xs.at[rows48(spot_t), half_cols(h)], S_T + 16 * h + i, (a, p)
            ).start()

    send_shares(0)
    normalise(zl * 8 + j)
    send_shares(1)
    hand_on(xa, mine, S_AG + 0, at_x(1), 0, NT).start()
    hand_on(xa, mine, S_AG + 1, at_x(-1), 0, NT).start()
    remote(xa.at[pl.ds(zl * 8, 8), mine, :], xc.at[:, mine, :], S_AG + 4, pair).start()
    xs[rows48(spot_t), :] = xa[zl * 8 + j, mine, :]

    names = jnp.broadcast_to(names_ref[...].astype(F32), (8, REQS)).astype(BF16)
    rr, cc = iota((REQS, GROUP), 0), iota((REQS, GROUP), 1)
    lane_spot = lax.shift_right_logical(lax.shift_right_logical(cc, 4) * 171, 9)
    lane_dev = (lane_spot & 3) * 4 + lax.shift_right_logical(lane_spot, 2)
    request = lane_dev * (ROWS // 4) + lax.shift_right_logical(cc - lane_spot * ROWS, 2)
    fourfold = jnp.where(rr == request, 1.0, 0.0).astype(BF16)
    tk[y] = jnp.dot(names, fourfold, preferred_element_type=F32).astype(I32)

    @pl.loop(1, NY)
    def _(i):
        remote(tk.at[y], tk.at[y], S_IDX + i, at_y(i)).start()

    local[3].wait()
    remote(kvb.at[0], kvb.at[1], S_KV, sibling).start()

    dest, slot = routing(tk[y, 0:1, :])

    @pl.loop(0, NY)
    def _(d):
        oh[d] = jnp.where(chosen(dest, slot, d), 1.0, 0.0).astype(BF16)

    def send_rows(h):
        @pl.loop(1, NT)
        def _(i):
            arrived(xs.at[rows48(0), half_cols(h)], S_T + 16 * h + i)

        @pl.loop(0, NY)
        def _(n):
            off = (order(n) + NY) % NY
            d = (y + off) % NY
            og[d, :, half_cols(h)] = jnp.dot(
                oh[d], xs[:, half_cols(h)], preferred_element_type=F32
            ).astype(BF16)

            @pl.when((n >= 1) & (n <= 3))
            def _():
                remote(
                    og.at[d, :, half_cols(h)], ig.at[y, :, half_cols(h)],
                    S_YA + 8 * h + off, (d * NZH + zh, t),
                ).start()

            @pl.when(off == 0)
            def _():
                ig[y, :, half_cols(h)] = og[d, :, half_cols(h)]

    local[4].wait()
    wd[zh] = dn[...].reshape(HELD * RANK, SHARE).T
    local[5].wait()
    for l in range(HELD):
        upd[zh, :, l * RANK : (l + 1) * RANK] = ups[l]

    top, low = pl.ds(0, SHARE // 2), pl.ds(SHARE // 2, SHARE // 2)

    def weights_on(q, part_of, i, to):
        ref = wd.at[(q + NZH) % NZH, part_of, :]
        remote(ref, ref, S_W + i, at_z(to)).start()

    weights_on(zh, top, 0, 1)
    weights_on(zh, low, 1, -1)
    weights_on(zh, low, 2, 1)
    weights_on(zh, top, 3, -1)

    send_rows(0)

    send_rows(1)


    def other_rows(core):
        return pl.ds(pl.multiple_of(((1 - zl) * 2 + core) * 4 * ROWS, 16), 4 * ROWS)

    @pl.loop(1, 8)
    def _(i):
        p = (j + i) % 8
        remote(
            xs.at[other_rows(p % 2), :], xb.at[j], S_XB + i, (a, tensor_of(p, zl))
        ).start()

    xb[j] = xs[other_rows(c), :]

    @pl.loop(1, NY)
    def _(i):
        arrived(tk.at[(y - i + NY) % NY], S_IDX + i)

    @pl.loop(0, NY)
    def _(g):
        their = tk[g, 0:1, :]
        to_row, at_slot = routing(their)
        held = (their & (NZH * HELD - 1)).astype(F32)
        lid = jnp.sum(
            jnp.where(chosen(to_row, at_slot, y), held, 0.0), axis=1, keepdims=True
        )
        wide = jnp.broadcast_to(lid, (CAP, 128)).astype(I32)
        lidb[g] = wide
        key = wide - lax.shift_right_logical(iota((CAP, 128), 1), 6)
        for k in range(NZH * 4):
            mask[g, k] = jnp.where(key == 2 * k, 1.0, 0.0).astype(BF16)

    arrived(wd.at[zh, top, :], S_W + 0)
    weights_on(zh - 1, top, 4, 1)
    arrived(wd.at[zh, low, :], S_W + 1)
    weights_on(zh + 1, low, 5, -1)

    for i in range(1, NZH):
        remote(upd.at[zh], upd.at[zh], S_UP + i, at_z(i)).start()


    for h in range(2):
        for off in (4, 3, 5):
            sent(og.at[0, :, half_cols(h)], S_YA + 8 * h + off)
    for off in (2, 6, 1, 7):
        d = (y + off) % NY
        remote(og.at[d], ig.at[y], S_YA + off, (d * NZH + zh, t)).start()

    arrived(xa.at[:, block(x - 1), :], S_AG + 0)
    hand_on(xa, block(x - 1), S_AG + 2, at_x(1), 0, 8).start()
    arrived(xa.at[:, block(x + 1), :], S_AG + 1)
    hand_on(xa, block(x + 1), S_AG + 3, at_x(-1), 8, 8).start()

    place = dest * HALF + jnp.where(slot < HALF, slot, slot - HALF)
    code = (place + jnp.where(slot < HALF, 0, 1024)).astype(F32)
    rr, cc = iota((GROUP, GROUP), 0), iota((GROUP, GROUP), 1)
    code_col = jnp.sum(jnp.where(rr == cc, code, 0.0), axis=1, keepdims=True).astype(I32)
    oht[0] = jnp.where(code_col == cc, 1.0, 0.0).astype(BF16)
    oht[1] = jnp.where(code_col == cc + 1024, 1.0, 0.0).astype(BF16)

    def weights(s):
        ks = pl.ds(pl.multiple_of(tensor_of(s % 8, s // 8) * SHARE, SHARE), SHARE)
        return jnp.concatenate([kvb[0, ks, :], kvb[1, ks, :]], axis=1)

    def base(buf, plane, many, at, fresh):
        at = pl.ds(pl.multiple_of(at * 4 * ROWS, 16), 4 * ROWS)

        def add(s, acc):
            return acc + jnp.dot(buf[s], weights(plane * 8 + s), preferred_element_type=F32)

        acc = lax.fori_loop(0, many, add, jnp.zeros((4 * ROWS, 256), F32))
        if fresh:
            bown[at, :] = acc[:, :128]
            bsend[at, :] = acc[:, 128:]
        else:
            bown[at, :] = bown[at, :] + acc[:, :128]
            bsend[at, :] = bsend[at, :] + acc[:, 128:]

    arrived(xc.at[:, mine, :], S_AG + 4)
    hand_on(xc, mine, S_AG + 5, at_x(1), 0, 8).start()
    hand_on(xc, mine, S_AG + 6, at_x(-1), 0, 8).start()

    arrived(kvb.at[1], S_KV)
    arrived(xa.at[pl.ds(0, 8), block(x + 2), :], S_AG + 2)
    arrived(xa.at[pl.ds(8, 8), block(x + 2), :], S_AG + 3)
    base(xa, 0, NT, zl, True)

    for i in range(2, 6):
        arrived(wd.at[zh, top, :], S_W + i)

    lane_low = iota((HALF, 128), 1) < RANK

    def source(n):
        off = (order(n) + NY) % NY
        return off, (y - off + NY) % NY

    def shrink(n):
        off, g = source(n)

        @pl.when((n >= 1) & (n <= 3))
        def _():
            for h in range(2):
                arrived(ig.at[g, :, half_cols(h)], S_YA + 8 * h + off)

        @pl.when(n >= 4)
        def _():
            arrived(ig.at[g], S_YA + off)

        lid = lidb[g]
        lid2 = lax.shift_right_logical(lid, 1)
        rows = ig[g]
        acc = jnp.zeros((CAP, 128), F32)
        for q in range(NZH):
            prod = jnp.dot(rows, wd[q], preferred_element_type=F32)
            for k in range(4):
                acc = jnp.where(lid2 == q * 4 + k, prod[:, 128 * k : 128 * k + 128], acc)
        part[g] = packed_rows(acc, lid).astype(BF16)
        for h in range(2):
            p = g * 2 + h
            i = (p - t + NT) % NT

            @pl.when(i != 0)
            def _():
                remote(
                    part.at[g, pl.ds(h * ROWS, ROWS), :], rsb.at[t], S_RS + i, (a, p)
                ).start()

            @pl.when(i == 0)
            def _():
                rsb[t] = part[g, h * ROWS : (h + 1) * ROWS, :]

    def own_sum():
        @pl.loop(1, NT)
        def _(i):
            arrived(rsb.at[(t - i + NT) % NT], S_RS + i)

        shrunk = lax.fori_loop(
            0, NT, lambda s, acc: acc + rsb[s].astype(F32), jnp.zeros((ROWS, 128), F32)
        )
        sh[rows48(t), :] = shrunk.astype(BF16)

        @pl.loop(1, NT)
        def _(i):
            remote(sh.at[rows48(t), :], sh.at[rows48(t), :], S_SH + i, at_tensor(i)).start()

    def expand(n):
        off, g = source(n)
        for h in range(2):
            p = g * 2 + h
            i = (t - p + NT) % NT

            @pl.when(i != 0)
            def _():
                arrived(sh.at[rows48(p), :], S_SH + i)

        spot = pl.ds(pl.multiple_of(g * HALF, 16), HALF)
        packed = sh[spot, :].astype(F32)
        turned = pltpu.roll(packed, RANK, 1)
        both = jnp.concatenate(
            [jnp.where(lane_low, packed, turned), jnp.where(lane_low, turned, packed)], axis=0
        ).astype(BF16)
        acc = jnp.zeros((CAP, 128), F32)
        for q in range(NZH):
            spread = jnp.concatenate([both * mask[g, q * 4 + k] for k in range(4)], axis=1)
            acc = acc + jnp.dot(spread, up2[q], preferred_element_type=F32)
        acc = acc * SCALE
        delta[g] = jnp.where(lane_low, acc[:HALF], acc[HALF:]).astype(BF16)

        @pl.when(off != 0)
        def _():
            remote(
                delta.at[g],
                dl.at[pl.ds(pl.multiple_of(y * HALF, 16), HALF), :],
                S_RET + (NY - off) % NY,
                (g * NZH + zh, t),
            ).start()

        @pl.when(off == 0)
        def _():
            dl[spot, :] = delta[g]

    apart = (y - t // 2 + NY) % NY
    beyond = apart // 4
    turn = beyond * (2 * apart - 7) + (1 - beyond) * (8 - 2 * apart) - 8 * ((7 - apart) // 7)
    LATE, LATER = 3, 5

    @pl.loop(0, NY + LATER)
    def _(n):
        @pl.when(n < NY)
        def _():
            shrink(n)

        @pl.when(n == 7)
        def _():
            arrived(xc.at[:, block(x - 1), :], S_AG + 5)
            hand_on(xc, block(x - 1), S_AG + 7, at_x(1), 0, 4).start()
            arrived(xc.at[:, block(x + 1), :], S_AG + 6)
            hand_on(xc, block(x + 1), S_AG + 8, at_x(-1), 4, 4).start()

        @pl.when(n == NY)
        def _():
            @pl.loop(1, 8)
            def _(i):
                arrived(xb.at[0], S_XB + i)

            base(xb, zl, 8, 1 - zl, True)

        @pl.when(n == turn + LATE - (turn // 6) * (turn - 5))
        def _():
            own_sum()

        @pl.when(n == LATER)
        def _():
            for i in range(1, NZH):
                arrived(upd.at[(zh - i + NZH) % NZH], S_UP + i)
            for q in range(NZH):
                for l in range(HELD):
                    piece = upd[q, :, l * RANK : (l + 1) * RANK]
                    up2[q, l * RANK : (l + 1) * RANK, 0:RANK] = piece
                    up2[q, l * RANK : (l + 1) * RANK, RANK : 2 * RANK] = piece

        @pl.when(n >= LATER)
        def _():
            expand(n - LATER)

    arrived(xc.at[pl.ds(0, 4), block(x + 2), :], S_AG + 7)
    arrived(xc.at[pl.ds(4, 4), block(x + 2), :], S_AG + 8)
    base(xc, 1 - zl, 8, 1 - zl, False)
    remote(bsend, bx, S_BX, sibling).start()

    @pl.loop(1, NY)
    def _(i):
        arrived(dl.at[pl.ds(pl.multiple_of(((y - i + NY) % NY) * HALF, 16), HALF), :], S_RET + i)

    arrived(bx, S_BX)

    upper_lane = iota((4 * ROWS, 128), 1) >= RANK

    @pl.loop(0, 4)
    def _(b):
        span = pl.ds(pl.multiple_of(b * 4 * ROWS, 16), 4 * ROWS)
        first = jnp.dot(oht[0, span, :], dl[...], preferred_element_type=F32)
        second = jnp.dot(oht[1, span, :], dl[...], preferred_element_type=F32)
        td = jnp.where(upper_lane, pltpu.roll(first, RANK, 1) + second, 0.0)
        rows = pl.ds(pl.multiple_of((b // 2) * 4 * ROWS, 16), 4 * ROWS)
        value = jnp.where(b % 2 == c, bown[rows, :], bx[rows, :]) + td
        for ix in range(NX):
            out_ref[rows48(ix * 4 + b), :] = value[ix * ROWS : (ix + 1) * ROWS].astype(BF16)

    @pl.loop(1, NT)
    def _(i):
        for h in range(2):
            sent(xa.at[0, mine, half_cols(h)], S_T + 16 * h + i)
        sent(part.at[0, pl.ds(0, ROWS), :], S_RS + i)
        sent(sh.at[rows48(t), :], S_SH + i)

    @pl.loop(1, NY)
    def _(i):
        sent(tk.at[y], S_IDX + i)
        sent(delta.at[0], S_RET + i)
        sent(xb.at[0], S_XB + i)

    for off in (1, 2, 6, 7):
        sent(og.at[0], S_YA + off)
    sent(kvb.at[0], S_KV)
    sent(bsend, S_BX)
    sent(xa.at[:, mine, :], S_AG + 0)
    sent(xa.at[:, mine, :], S_AG + 1)
    for i in (2, 3, 4, 5, 6):
        sent(xc.at[:, mine, :], S_AG + i)
    for i in (7, 8):
        sent(xc.at[pl.ds(0, 4), mine, :], S_AG + i)
    for i in range(6):
        sent(wd.at[zh, top, :], S_W + i)
    for i in range(1, NZH):
        sent(upd.at[zh], S_UP + i)


def per_device(residual, gain, kv, down, up, names):
    hbm = pl.BlockSpec(memory_space=pltpu.HBM)
    vmem = pl.BlockSpec(memory_space=pltpu.VMEM)
    V = pltpu.VMEM
    return pl.pallas_call(
        kernel,
        name="lora_kv",
        out_shape=jax.ShapeDtypeStruct((GROUP, 128), BF16),
        in_specs=[hbm] * 6,
        out_specs=vmem,
        scratch_shapes=[
            V((ROWS, WIDTH), BF16),
            V((WIDTH,), BF16),
            V((1, REQS), I32),
            V((NT, NX * ROWS, SHARE), BF16),
            V((8, NX * ROWS, SHARE), BF16),
            V((8, NX * ROWS, SHARE), BF16),
            V((GROUP, SHARE), BF16),
            V((2, WIDTH, 128), BF16),
            V((HELD, RANK, SHARE), BF16),
            V((NZH, SHARE, HELD * RANK), BF16),
            V((HELD, RANK, RANK), BF16),
            V((NZH, RANK, HELD * RANK), BF16),
            V((NZH, HELD * RANK, 128), BF16),
            V((NY, NZH * 4, CAP, 128), BF16),
            V((NY, CAP, GROUP), BF16),
            V((2, GROUP, GROUP), BF16),
            V((NY, CAP, SHARE), BF16),
            V((NY, CAP, SHARE), BF16),
            V((NY, HALF, 128), BF16),
            V((NY, 8, GROUP), I32),
            V((NY, CAP, 128), I32),
            V((NY, HALF, 128), BF16),
            V((NT, ROWS, 128), BF16),
            V((GROUP, 128), BF16),
            V((GROUP, 128), BF16),
            V((GROUP // 2, 128), F32),
            V((GROUP // 2, 128), F32),
            V((GROUP // 2, 128), F32),
            pltpu.SemaphoreType.DMA((N_SEM,)),
            pltpu.SemaphoreType.DMA((N_SEM,)),
            pltpu.SemaphoreType.DMA((6,)),
        ],
        compiler_params=pltpu.CompilerParams(
            collective_id=0, has_side_effects=True, vmem_limit_bytes=63 << 20
        ),
    )(residual, gain, kv, jnp.swapaxes(down, 1, 2), up, names.reshape(1, REQS))


def solution(mesh):
    in_specs = (
        P(("adapter", "tensor"), None),
        P(),
        P(None, "tensor"),
        P("adapter", "tensor", None),
        P("adapter", None, "tensor"),
        P("adapter", None),
    )
    return jax.shard_map(
        per_device,
        mesh=mesh,
        in_specs=in_specs,
        out_specs=P("adapter", "tensor"),
        check_vma=False,
    )
```
